32 devices in a mesh: dp: 8 (over z, x), tensor: 4 (over y, core).
Axes of the slice: x: 2, y: 2, z: 4, core: 2. Of those that a mesh axis runs over, the one named last changes fastest.
Arguments:
- inputs: bfloat16 [8, 128, 8192], P('dp'), may hold values from -6 to 6
- x_pre: bfloat16 [8, 128, 4096], P('dp', None, 'tensor'), may hold values from -6 to 6
- bc_pre: bfloat16 [8, 128, 512], P('dp', None, 'tensor'), may hold values from -6 to 6
- dt_pre: float32 [8, 128, 64], P('dp', None, 'tensor'), may hold values from -3 to 3
- gate_in: bfloat16 [8, 128, 4096], P('dp', None, 'tensor'), may hold values from -6 to 6
- conv_x: float32 [4, 4096], P(None, 'tensor'), may hold values from -3 to 3
- conv_bc: float32 [4, 512], P(None, 'tensor'), may hold values from -3 to 3
- dt_bias: float32 [64], P('tensor'), may hold values from -4 to -2
- a_log: float32 [64], P('tensor'), may hold values from -4.5 to 0
- d_skip: float32 [64], P('tensor'), may hold values from 0.5 to 1.5
- norm_w: float32 [4096], P('tensor'), may hold values from 0.5 to 1.5
- out_grad: bfloat16 [8, 128, 4096], P('dp', None, 'tensor'), may hold values from -6 to 6
- w_x: bfloat16 [8192, 4096], P('dp', 'tensor'), may hold values from -0.0625 to 0.0625
- w_bc: bfloat16 [8192, 512], P('dp', 'tensor'), may hold values from -0.0625 to 0.0625
- w_dt: bfloat16 [8192, 64], P('dp', 'tensor'), may hold values from -0.0625 to 0.0625
Outputs:
- g_inputs: bfloat16 [8, 128, 8192], P('dp', None, 'tensor')
- g_gate: bfloat16 [8, 128, 4096], P('dp', None, 'tensor')
- g_wx: bfloat16 [8192, 4096], P('dp', 'tensor')
- g_wbc: bfloat16 [8192, 512], P('dp', 'tensor')
- g_wdt: bfloat16 [8192, 64], P('dp', 'tensor')
- g_convx: float32 [4, 4096], P(None, 'tensor')
- g_convbc: float32 [4, 512], P(None, 'tensor')
- g_dtbias: float32 [64], P('tensor')
- g_alog: float32 [64], P('tensor')
- g_dskip: float32 [64], P('tensor')
- g_normw: float32 [4096], P('tensor')
The draws below stay inside these ranges and needn't reach their ends.
All inputs are finite; a program needn't handle non-finite values.
Results may differ from the reference program's by a relative error of at most 0.015.
Values may be sent and summed in bfloat16 or wider, within the bound.
A program may use at most 128 MiB of HBM per device.

```python
import jax
import jax.numpy as jnp
from jax import lax

MODEL = 8192
HEAD_DIM = 64
HEADS_DEV = 16
STATE = 128
KERNEL = 4
LEN = 128
SEQS = 8
HEADS = 64
INNER = 4096
BCW = 512
N_TENSOR = 4


def level_of(key, shape, shards, low, top_value):
    def one(dim, parts):
        steps = jax.random.uniform(jax.random.fold_in(jax.random.fold_in(key, 6), dim), (parts,), jnp.float32, low / len(shards), top_value / len(shards))
        return jnp.repeat(jnp.exp(steps), shape[dim] // parts).reshape((-1,) + (1,) * (len(shape) - dim - 1))

    loudness = one(*shards[0])
    for cut in shards[1:]:
        loudness = loudness * one(*cut)
    return loudness


def scatter_about(rng, dims, width, most, split=(), kind=jnp.bfloat16):
    drawn = width * jax.random.normal(rng, dims, jnp.float32)
    if split:
        drawn = drawn * level_of(rng, dims, split, -0.22, 0.18)
    return jnp.clip(drawn, -most, most).astype(kind)


def setup_inputs(seed: int = 0) -> dict:
    arg_keys = jax.random.split(jax.random.key(seed), 16)
    inputs = scatter_about(arg_keys[0], (SEQS, LEN, MODEL), 1.0, 6.0, ((0, 8),))
    x_pre = scatter_about(arg_keys[1], (SEQS, LEN, INNER), 1.0, 6.0, ((0, 8), (2, 4)))
    bc_pre = scatter_about(arg_keys[2], (SEQS, LEN, BCW), 1.0, 6.0, ((0, 8), (2, 4)))
    dt_pre = scatter_about(arg_keys[3], (SEQS, LEN, HEADS), 0.5, 3.0, ((0, 8), (2, 4)), jnp.float32)
    gate_in = scatter_about(arg_keys[4], (SEQS, LEN, INNER), 1.0, 6.0, ((0, 8), (2, 4)))
    conv_x = scatter_about(arg_keys[5], (KERNEL, INNER), KERNEL ** -0.5, 3.0, ((1, 4),), jnp.float32)
    conv_bc = scatter_about(arg_keys[6], (KERNEL, BCW), KERNEL ** -0.5, 3.0, ((1, 4),), jnp.float32)
    dt_bias = jnp.clip(-4.0 + 2.0 * jax.random.uniform(arg_keys[7], (HEADS,), jnp.float32) ** level_of(arg_keys[7], (HEADS,), ((0, 4),), -0.2, 0.2), -4.0, -2.0)
    a_log = jnp.clip(-4.5 + 4.5 * jax.random.uniform(arg_keys[8], (HEADS,), jnp.float32) ** level_of(arg_keys[8], (HEADS,), ((0, 4),), -0.2, 0.2), -4.5, 0.0)
    d_skip = jnp.clip(0.5 + 1.0 * jax.random.uniform(arg_keys[9], (HEADS,), jnp.float32) ** level_of(arg_keys[9], (HEADS,), ((0, 4),), -0.2, 0.2), 0.5, 1.5)
    norm_w = jnp.clip(1.0 + 0.1 * jax.random.normal(arg_keys[10], (INNER,), jnp.float32), 0.5, 1.5)
    out_grad = scatter_about(arg_keys[11], (SEQS, LEN, INNER), 1.0, 6.0, ((0, 8), (2, 4)))
    w_x = scatter_about(arg_keys[12], (MODEL, INNER), MODEL ** -0.5, 0.0625, ((0, 8), (1, 4)))
    w_bc = scatter_about(arg_keys[13], (MODEL, BCW), MODEL ** -0.5, 0.0625, ((0, 8), (1, 4)))
    w_dt = scatter_about(arg_keys[14], (MODEL, HEADS), MODEL ** -0.5, 0.0625, ((0, 8), (1, 4)))
    return {"inputs": inputs, "x_pre": x_pre, "bc_pre": bc_pre, "dt_pre": dt_pre, "gate_in": gate_in, "conv_x": conv_x, "conv_bc": conv_bc, "dt_bias": dt_bias, "a_log": a_log, "d_skip": d_skip, "norm_w": norm_w, "out_grad": out_grad, "w_x": w_x, "w_bc": w_bc, "w_dt": w_dt}


EPSILON = 1e-05
PRECISE = lax.Precision.HIGHEST

def causal_conv(values, kernel):
    kernel_width = kernel.shape[0]
    seq_len = values.shape[0]
    padded = jnp.pad(values, ((kernel_width - 1, 0), (0, 0)))
    running = jnp.zeros(values.shape, jnp.float32)
    for offset in range(kernel_width):
        running = running + kernel[offset] * padded[offset:offset + seq_len]
    return running

def state_act(pre_values, kernel):
    return jax.nn.silu(causal_conv(pre_values, kernel))

def state_mix(x_pre, b_mat, c_mat, dt_pre, gate_in, conv_x, dt_bias, a_log, d_skip):
    seq_len, channels = x_pre.shape
    head_count = dt_pre.shape[1]
    groups = b_mat.shape[1]
    per_group = head_count // groups
    head_size = channels // head_count
    mixed_x = jax.nn.silu(causal_conv(x_pre, conv_x))
    step_size = jax.nn.softplus(dt_pre + dt_bias)
    decay_rate = -jnp.exp(a_log)
    log_decay = jnp.cumsum(step_size * decay_rate, axis=0).T
    scores = jnp.einsum('tgn,sgn->gts', c_mat, b_mat, precision=PRECISE)
    scores = jnp.repeat(scores, per_group, axis=0)
    causal = jnp.arange(seq_len)[:, None] >= jnp.arange(seq_len)[None, :]
    decay_mat = jnp.exp(jnp.where(causal[None], log_decay[:, :, None] - log_decay[:, None, :], -jnp.inf))
    weights = scores * decay_mat * step_size.T[:, None, :]
    heads_x = mixed_x.reshape(seq_len, head_count, head_size)
    result = jnp.einsum('hts,shp->thp', weights, heads_x, precision=PRECISE) + d_skip[None, :, None] * heads_x
    return result.reshape(seq_len, channels) * jax.nn.silu(gate_in)

def norm_out(mixed_v, norm_w, groups):
    seq_len, channels = mixed_v.shape
    grouped = mixed_v.reshape(seq_len, groups, channels // groups)
    inv_rms = lax.rsqrt(lax.optimization_barrier(jnp.mean(grouped * grouped, axis=-1, keepdims=True)) + EPSILON)
    return (grouped * inv_rms).reshape(seq_len, channels) * norm_w

def reference(inputs, x_pre, bc_pre, dt_pre, gate_in, conv_x, conv_bc, dt_bias, a_log, d_skip, norm_w, out_grad, w_x, w_bc, w_dt):
    groups = N_TENSOR // 2
    channels = HEADS_DEV * HEAD_DIM
    part_count = N_TENSOR
    block_width = channels + STATE + HEADS_DEV
    w_cat = jnp.concatenate([w_x.reshape(MODEL, part_count, channels), w_bc.reshape(MODEL, part_count, STATE), w_dt.reshape(MODEL, part_count, HEADS_DEV)], axis=2)

    def forward(xp, b_mat, c_mat, dtp, gates, kernel, bias, alog, skip, gain):
        return norm_out(state_mix(xp, b_mat, c_mat, dtp, gates, kernel, bias, alog, skip), gain, groups)

    def one_seq(carry, seq_data):
        weight_acc, small = carry
        u_seq, x_seq, bcp_seq, dtp_seq, z_seq, g_seq = seq_data
        bc_pre32 = bcp_seq.astype(jnp.float32)
        bc_value = state_act(bc_pre32, conv_bc).astype(jnp.bfloat16)
        bc_float = lax.optimization_barrier(bc_value).astype(jnp.float32)
        quad_view = bc_float.reshape(LEN, groups, 2, STATE)
        _, pullback = jax.vjp(forward, x_seq.astype(jnp.float32), quad_view[:, :, 0], quad_view[:, :, 1], dtp_seq, z_seq.astype(jnp.float32), conv_x, dt_bias, a_log, d_skip, norm_w)
        grad_x, grad_b, grad_c, grad_dt, grad_z, grad_cx, grad_db, grad_al, grad_ds, grad_nw = pullback(g_seq.astype(jnp.float32))
        grad_bcact = jnp.stack([grad_b, grad_c], axis=2).reshape(LEN, groups * 2 * STATE)
        _, pull_conv = jax.vjp(state_act, bc_pre32, conv_bc)
        grad_bcp, grad_cbc = pull_conv(grad_bcact)
        g_cat = jnp.concatenate([grad_x.astype(jnp.bfloat16).reshape(LEN, part_count, channels), grad_bcp.astype(jnp.bfloat16).reshape(LEN, part_count, STATE), grad_dt.astype(jnp.bfloat16).reshape(LEN, part_count, HEADS_DEV)], axis=2)

        def add_part(running, index):
            g_block = lax.dynamic_index_in_dim(g_cat, index, 1, keepdims=False)
            w_block = lax.dynamic_index_in_dim(w_cat, index, 1, keepdims=False)
            term = jnp.dot(g_block, w_block.T, preferred_element_type=jnp.float32)
            return (running + lax.optimization_barrier(term.astype(jnp.bfloat16)).astype(jnp.float32), None)
        grad_in, _ = lax.scan(add_part, jnp.zeros((LEN, MODEL), jnp.float32), jnp.arange(part_count, dtype=jnp.int32))
        weight_term = jnp.dot(u_seq.T, g_cat.reshape(LEN, part_count * block_width), preferred_element_type=jnp.float32)
        weight_acc = weight_acc + lax.optimization_barrier(weight_term.astype(jnp.bfloat16)).astype(jnp.float32)
        small = jax.tree.map(lambda left, right: left + right, small, (grad_cx, grad_cbc, grad_db, grad_al, grad_ds, grad_nw))
        return ((weight_acc, small), (grad_in.astype(jnp.bfloat16), grad_z.astype(jnp.bfloat16)))
    small_init = (jnp.zeros(conv_x.shape, jnp.float32), jnp.zeros(conv_bc.shape, jnp.float32), jnp.zeros(dt_bias.shape, jnp.float32), jnp.zeros(a_log.shape, jnp.float32), jnp.zeros(d_skip.shape, jnp.float32), jnp.zeros(norm_w.shape, jnp.float32))
    init = (jnp.zeros((MODEL, part_count * block_width), jnp.float32), small_init)
    (weight_acc, small), (g_inputs, g_gate) = lax.scan(one_seq, init, (inputs, x_pre, bc_pre, dt_pre, gate_in, out_grad))
    weight_grad = weight_acc.astype(jnp.bfloat16).reshape(MODEL, part_count, block_width)
    g_wx = weight_grad[:, :, :channels].reshape(MODEL, part_count * channels)
    g_wbc = weight_grad[:, :, channels:channels + STATE].reshape(MODEL, part_count * STATE)
    g_wdt = weight_grad[:, :, channels + STATE:].reshape(MODEL, part_count * HEADS_DEV)
    return (g_inputs, g_gate, g_wx, g_wbc, g_wdt, small[0], small[1], small[2], small[3], small[4], small[5])
```

```python
import jax
import jax.numpy as jnp
from jax import lax
from jax.sharding import PartitionSpec as P

EPSILON = 1e-05
PRECISE = lax.Precision.HIGHEST


def swapped(block, axis, distance):
    count = lax.axis_size(axis)
    route = []
    for low in range(count):
        high = low | 1 << distance
        if high != low and high < count:
            route += [(low, high), (high, low)]
    return lax.ppermute(block, axis, route)


def causal_conv(values, kernel):
    kernel_width = kernel.shape[0]
    seq_len = values.shape[0]
    padded = jnp.pad(values, ((kernel_width - 1, 0), (0, 0)))
    running = jnp.zeros(values.shape, jnp.float32)
    for offset in range(kernel_width):
        running = running + kernel[offset] * padded[offset : offset + seq_len]
    return running


def state_act(pre_values, kernel):
    return jax.nn.silu(causal_conv(pre_values, kernel))


def state_mix(x_pre, b_mat, c_mat, dt_pre, gate_in, conv_x, dt_bias, a_log, d_skip):
    seq_len, channels = x_pre.shape
    head_count = dt_pre.shape[1]
    groups = b_mat.shape[1]
    per_group = head_count // groups
    head_size = channels // head_count
    mixed_x = jax.nn.silu(causal_conv(x_pre, conv_x))
    step_size = jax.nn.softplus(dt_pre + dt_bias)
    decay_rate = -jnp.exp(a_log)
    log_decay = jnp.cumsum(step_size * decay_rate, axis=0).T
    scores = jnp.einsum("tgn,sgn->gts", c_mat, b_mat, precision=PRECISE)
    scores = jnp.repeat(scores, per_group, axis=0)
    causal = jnp.arange(seq_len)[:, None] >= jnp.arange(seq_len)[None, :]
    decay_mat = jnp.exp(
        jnp.where(causal[None], log_decay[:, :, None] - log_decay[:, None, :], -jnp.inf)
    )
    weights = scores * decay_mat * step_size.T[:, None, :]
    heads_x = mixed_x.reshape(seq_len, head_count, head_size)
    result = (
        jnp.einsum("hts,shp->thp", weights, heads_x, precision=PRECISE)
        + d_skip[None, :, None] * heads_x
    )
    return result.reshape(seq_len, channels) * jax.nn.silu(gate_in)


def body(
    inputs,
    x_pre,
    bc_pre,
    dt_pre,
    gate_in,
    conv_x,
    conv_bc,
    dt_bias,
    a_log,
    d_skip,
    norm_w,
    out_grad,
    w_x,
    w_bc,
    w_dt,
):
    channels = x_pre.shape[2]
    half_width = bc_pre.shape[2]
    seq_len, model = inputs.shape[1:]
    dp_size, tensor_size = lax.axis_size("dp"), lax.axis_size("tensor")
    dp_rows = model // dp_size
    piece = dp_rows // tensor_size
    own_piece = lax.dynamic_index_in_dim(
        inputs[0].reshape(seq_len, dp_size, tensor_size, piece),
        lax.axis_index("tensor"), 2, keepdims=False,
    ).transpose(1, 0, 2)
    row_piece = lax.all_to_all(own_piece, "dp", 0, 0, tiled=True)
    row_pieces = lax.all_gather(
        row_piece.reshape(dp_size * seq_len, piece), "tensor", axis=0, tiled=False)
    is_even = lax.axis_index("tensor") % 2 == 0
    bc_pre32 = bc_pre[0].astype(jnp.float32)
    own_half = state_act(bc_pre32, conv_bc).astype(jnp.bfloat16)
    far_half = swapped(own_half, "tensor", 0)
    own_float = lax.optimization_barrier(own_half).astype(jnp.float32)
    far_float = far_half.astype(jnp.float32)
    b_mat = jnp.where(is_even, own_float, far_float)[:, None, :]
    c_mat = jnp.where(is_even, far_float, own_float)[:, None, :]
    mixed_v, pullback = jax.vjp(
        state_mix,
        x_pre[0].astype(jnp.float32),
        b_mat,
        c_mat,
        dt_pre[0],
        gate_in[0].astype(jnp.float32),
        conv_x,
        dt_bias,
        a_log,
        d_skip,
    )
    upstream = out_grad[0].astype(jnp.float32)
    scaled = upstream * norm_w
    own_stats = jnp.stack([jnp.sum(mixed_v * mixed_v, axis=1), jnp.sum(scaled * mixed_v, axis=1)])
    far_stats = swapped(own_stats, "tensor", 0)
    group_stats = (own_stats + far_stats) / (2 * channels)
    inv_rms = lax.rsqrt(group_stats[0] + EPSILON)[:, None]
    grad_v = inv_rms * scaled - mixed_v * (inv_rms * inv_rms * inv_rms) * group_stats[1][:, None]
    grad_x, grad_b, grad_c, grad_dt, grad_z, grad_cx, grad_db, grad_al, grad_ds = pullback(grad_v)
    kept_grad = jnp.where(is_even, grad_b[:, 0], grad_c[:, 0])
    sent_grad = jnp.where(is_even, grad_c[:, 0], grad_b[:, 0])
    grad_own = kept_grad + swapped(sent_grad.astype(jnp.bfloat16), "tensor", 0).astype(
        sent_grad.dtype
    )
    _, pull_conv = jax.vjp(state_act, bc_pre32, conv_bc)
    grad_bcp, grad_cbc = pull_conv(grad_own)
    norm_part = jnp.sum(upstream * mixed_v * inv_rms, axis=0)
    heads = dt_pre.shape[2]
    short = jnp.pad(
        jnp.concatenate([grad_cbc.reshape(-1), grad_db, grad_al, grad_ds]),
        (0, -(4 * half_width + 3 * heads) % channels)).reshape(-1, channels)
    packed = jnp.concatenate([grad_cx, norm_part[None], short], axis=0)
    packed = jnp.sum(lax.all_gather(packed, "dp", axis=0, tiled=False), axis=0)
    taps = grad_cx.shape[0]
    flat = packed[taps + 1 :].reshape(-1)
    cut = taps * half_width
    param_grads = (
        packed[:taps],
        flat[:cut].reshape(taps, half_width),
        flat[cut : cut + heads],
        flat[cut + heads : cut + 2 * heads],
        flat[cut + 2 * heads : cut + 3 * heads],
        packed[taps],
    )
    g_cat = jnp.concatenate(
        [grad_x.astype(jnp.bfloat16), grad_bcp.astype(jnp.bfloat16), grad_dt.astype(jnp.bfloat16)],
        axis=1,
    )
    g_all = lax.all_gather(g_cat, "dp", axis=0, tiled=True)
    w_cat = jnp.concatenate([w_x, w_bc, w_dt], axis=1)
    partial_in = lax.dot_general(
        g_all, w_cat, (((1,), (1,)), ((), ())), preferred_element_type=jnp.float32
    ).astype(jnp.bfloat16)
    part = seq_len // tensor_size
    summed = lax.psum_scatter(
        partial_in.reshape(dp_size, tensor_size, part, dp_rows).transpose(1, 0, 2, 3)
        .reshape(tensor_size * dp_size * part, dp_rows),
        "tensor", scatter_dimension=0, tiled=True)
    moved = lax.all_to_all(summed.reshape(dp_size, part, dp_rows), "dp", 0, 0, tiled=True)
    moved = moved.transpose(1, 0, 2).reshape(part, tensor_size, model // tensor_size)
    moved = lax.all_to_all(moved.transpose(1, 0, 2), "tensor", 0, 0, tiled=True)
    grad_in = moved.reshape(1, seq_len, model // tensor_size)
    grad_w = lax.dot_general(
        row_pieces, g_all, (((1,), (0,)), ((), ())), preferred_element_type=jnp.float32
    ).astype(jnp.bfloat16).reshape(dp_rows, -1)
    return (
        grad_in,
        grad_z.astype(jnp.bfloat16)[None],
        grad_w[:, :channels],
        grad_w[:, channels : channels + half_width],
        grad_w[:, channels + half_width :],
        param_grads[0],
        param_grads[1],
        param_grads[2],
        param_grads[3],
        param_grads[4],
        param_grads[5],
    )


def solution(mesh):
    placed = (
        P("dp", None, None),
        P("dp", None, "tensor"),
        P("dp", None, "tensor"),
        P("dp", None, "tensor"),
        P("dp", None, "tensor"),
        P(None, "tensor"),
        P(None, "tensor"),
        P("tensor"),
        P("tensor"),
        P("tensor"),
        P("tensor"),
        P("dp", None, "tensor"),
        P("dp", "tensor"),
        P("dp", "tensor"),
        P("dp", "tensor"),
    )
    return jax.shard_map(
        body,
        mesh=mesh,
        in_specs=placed,
        out_specs=(
            P("dp", None, "tensor"),
            P("dp", None, "tensor"),
            P("dp", "tensor"),
            P("dp", "tensor"),
            P("dp", "tensor"),
            P(None, "tensor"),
            P(None, "tensor"),
            P("tensor"),
            P("tensor"),
            P("tensor"),
            P("tensor"),
        ),
        check_vma=False,
    )
```

```python
import jax
import jax.numpy as jnp
from jax import lax
from jax.experimental import pallas as pl
from jax.experimental.pallas import tpu as pltpu
from jax.sharding import PartitionSpec as P
import functools

EPSILON = 1e-05
PRECISE = lax.Precision.HIGHEST


def swapped(block, axis, distance):
    count = lax.axis_size(axis)
    route = []
    for low in range(count):
        high = low | 1 << distance
        if high != low and high < count:
            route += [(low, high), (high, low)]
    return lax.ppermute(block, axis, route)


def causal_conv(values, kernel):
    kernel_width = kernel.shape[0]
    seq_len = values.shape[0]
    padded = jnp.pad(values, ((kernel_width - 1, 0), (0, 0)))
    running = jnp.zeros(values.shape, jnp.float32)
    for offset in range(kernel_width):
        running = running + kernel[offset] * padded[offset : offset + seq_len]
    return running


def state_act(pre_values, kernel):
    return jax.nn.silu(causal_conv(pre_values, kernel))


def state_mix(x_pre, b_mat, c_mat, dt_pre, gate_in, conv_x, dt_bias, a_log, d_skip):
    seq_len, channels = x_pre.shape
    head_count = dt_pre.shape[1]
    groups = b_mat.shape[1]
    per_group = head_count // groups
    head_size = channels // head_count
    mixed_x = jax.nn.silu(causal_conv(x_pre, conv_x))
    step_size = jax.nn.softplus(dt_pre + dt_bias)
    decay_rate = -jnp.exp(a_log)
    log_decay = jnp.cumsum(step_size * decay_rate, axis=0).T
    scores = jnp.einsum("tgn,sgn->gts", c_mat, b_mat, precision=PRECISE)
    scores = jnp.repeat(scores, per_group, axis=0)
    causal = jnp.arange(seq_len)[:, None] >= jnp.arange(seq_len)[None, :]
    decay_mat = jnp.exp(
        jnp.where(causal[None], log_decay[:, :, None] - log_decay[:, None, :], -jnp.inf)
    )
    weights = scores * decay_mat * step_size.T[:, None, :]
    heads_x = mixed_x.reshape(seq_len, head_count, head_size)
    result = (
        jnp.einsum("hts,shp->thp", weights, heads_x, precision=PRECISE)
        + d_skip[None, :, None] * heads_x
    )
    return result.reshape(seq_len, channels) * jax.nn.silu(gate_in)


def ring_index(place, count):
    place = lax.rem(place + 2 * count, count)
    return jnp.where(place < count // 2, 2 * place, 2 * (count - 1 - place) + 1)


def exchange_kernel(
    n, m, g_ref, w_ref, q_ref, all_ref, sum_ref, out_ref,
    part_buf, far_buf, red_buf, q_buf,
    ring_send, ring_recv, q_send, q_recv, far_send, far_recv, red_send, red_recv,
):
    d, t = lax.axis_index("dp"), lax.axis_index("tensor")
    seq_len = g_ref.shape[0]
    part = seq_len // m
    ratio = n // m
    goal = d // ratio
    column = lax.rem(d, ratio)
    place = jnp.where(lax.rem(d, 2) == 0, d // 2, n - 1 - d // 2)
    right, left = ring_index(place + 1, n), ring_index(place - 1, n)
    right_steps = n // 2
    left_steps = n - 1 - right_steps
    barrier = pltpu.get_barrier_semaphore()

    def signal(dp, tensor):
        pl.semaphore_signal(
            barrier, inc=1, device_id={"dp": dp, "tensor": tensor},
            device_id_type=pl.DeviceIdType.MESH)

    def greet_dp(k, c):
        signal(lax.rem(d + k, n), t)
        return c

    def greet_tensor(k, c):
        signal(d, lax.rem(t + k, m))
        return c

    def greet_out(s, c):
        @pl.when(jnp.logical_or(s != d, goal != t))
        def _():
            signal(s, goal)
        return c

    def greet_in(i, c):
        source, other = t * ratio + i // m, lax.rem(i, m)

        @pl.when(jnp.logical_or(source != d, other != t))
        def _():
            signal(source, other)
        return c

    lax.fori_loop(1, n, greet_dp, 0)
    lax.fori_loop(1, m, greet_tensor, 0)
    lax.fori_loop(0, n, greet_out, 0)
    lax.fori_loop(0, ratio * m, greet_in, 0)
    all_ref[0] = g_ref[...]
    q_buf[0] = q_ref[...]
    is_self = (goal == t).astype(jnp.int32)
    pl.semaphore_wait(barrier, (n - 1) + (m - 1) + n + ratio * m - 2 * is_self)

    def q_copy(k):
        return pltpu.make_async_remote_copy(
            src_ref=q_ref, dst_ref=q_buf.at[k], send_sem=q_send.at[k], recv_sem=q_recv.at[k],
            device_id={"dp": lax.rem(d + k, n)}, device_id_type=pl.DeviceIdType.MESH)

    def ring_copy(way, k):
        source = ring_index(place - k if way == 0 else place + k, n)
        target = right if way == 0 else left
        return pltpu.make_async_remote_copy(
            src_ref=all_ref.at[lax.rem(d - source + n, n)],
            dst_ref=all_ref.at[lax.rem(target - source + n, n)],
            send_sem=ring_send.at[way, k], recv_sem=ring_recv.at[way, k],
            device_id={"dp": target}, device_id_type=pl.DeviceIdType.MESH)

    def far_copy(j, k):
        other = lax.rem(t + k, m)
        return pltpu.make_async_remote_copy(
            src_ref=part_buf.at[j, other], dst_ref=far_buf.at[j, k],
            send_sem=far_send.at[j, k], recv_sem=far_recv.at[j, k],
            device_id={"tensor": other}, device_id_type=pl.DeviceIdType.MESH)

    def out_copy(j, s):
        return pltpu.make_async_remote_copy(
            src_ref=red_buf.at[j], dst_ref=out_ref.at[column, t],
            send_sem=red_send.at[j], recv_sem=red_recv.at[column, t],
            device_id={"dp": s, "tensor": goal}, device_id_type=pl.DeviceIdType.MESH)

    def source_of(j):
        k = (j + 1) // 2
        return ring_index(jnp.where(lax.rem(j, 2) == 1, place - k, place + k), n)

    def is_remote(s):
        return jnp.logical_or(s != d, goal != t)

    ring_copy(0, 0).start()
    ring_copy(1, 0).start()

    def q_start(k, c):
        q_copy(k).start()
        return c

    lax.fori_loop(1, n, q_start, 0)

    def reduce(j):
        total = part_buf[j, t].astype(jnp.float32)
        for k in range(1, m):
            far_copy(j, k).wait_recv()
            total = total + far_buf[j, k].astype(jnp.float32)
        red_buf[j] = total.astype(jnp.bfloat16)
        s = source_of(j)

        @pl.when(is_remote(s))
        def _():
            out_copy(j, s).start()

        @pl.when(jnp.logical_not(is_remote(s)))
        def _():
            out_ref[column, t] = red_buf[j]

    def step(j, c):
        k = j // 2

        @pl.when(lax.rem(j, 2) == 1)
        def _():
            ring_copy(0, k).wait_recv()

            @pl.when(k + 1 < right_steps)
            def _():
                ring_copy(0, k + 1).start()

        @pl.when(jnp.logical_and(lax.rem(j, 2) == 0, j > 0))
        def _():
            ring_copy(1, k - 1).wait_recv()

            @pl.when(k < left_steps)
            def _():
                ring_copy(1, k).start()

        slot = lax.rem(d - source_of(j) + n, n)
        product = lax.dot_general(
            all_ref[slot], w_ref[...], (((1,), (1,)), ((), ())),
            preferred_element_type=jnp.float32)
        part_buf[j] = product.reshape(m, part, product.shape[1]).astype(jnp.bfloat16)
        for hop in range(1, m):
            far_copy(j, hop).start()

        @pl.when(j > 0)
        def _():
            reduce(j - 1)
        return c

    lax.fori_loop(0, n, step, 0)
    reduce(n - 1)

    def q_finish(k, c):
        q_copy(k).wait()
        return c

    lax.fori_loop(1, n, q_finish, 0)
    sum_ref[...] = jnp.sum(q_buf[...], axis=0)
    for k in range(right_steps):
        ring_copy(0, k).wait_send()
    for k in range(left_steps):
        ring_copy(1, k).wait_send()

    def drain(j, c):
        for k in range(1, m):
            far_copy(j, k).wait_send()
        s = source_of(j)

        @pl.when(is_remote(s))
        def _():
            out_copy(j, s).wait_send()
        return c

    lax.fori_loop(0, n, drain, 0)

    def arrive(i, c):
        r, other = i // m, lax.rem(i, m)

        @pl.when(jnp.logical_or(t * ratio + r != d, other != t))
        def _():
            pltpu.make_async_remote_copy(
                src_ref=red_buf.at[0], dst_ref=out_ref.at[r, other],
                send_sem=red_send.at[0], recv_sem=red_recv.at[r, other],
                device_id={"dp": t * ratio + r, "tensor": other},
                device_id_type=pl.DeviceIdType.MESH).wait_recv()
        return c

    lax.fori_loop(0, ratio * m, arrive, 0)


def exchange(g_cat, w_cat, packed, n, m):
    seq_len, width = g_cat.shape
    rows = w_cat.shape[0]
    part = seq_len // m
    vmem = pl.BlockSpec(memory_space=pltpu.VMEM)
    dma = pltpu.SemaphoreType.DMA
    return pl.pallas_call(
        functools.partial(exchange_kernel, n, m),
        out_shape=(
            jax.ShapeDtypeStruct((n, seq_len, width), jnp.bfloat16),
            jax.ShapeDtypeStruct(packed.shape, jnp.float32),
            jax.ShapeDtypeStruct((n // m, m, part, rows), jnp.bfloat16),
        ),
        in_specs=[vmem] * 3,
        out_specs=[vmem] * 3,
        scratch_shapes=[
            pltpu.VMEM((n, m, part, rows), jnp.bfloat16),
            pltpu.VMEM((n, m, part, rows), jnp.bfloat16),
            pltpu.VMEM((n, part, rows), jnp.bfloat16),
            pltpu.VMEM((n,) + packed.shape, jnp.float32),
            dma((2, n)), dma((2, n)), dma((n,)), dma((n,)),
            dma((n, m)), dma((n, m)), dma((n,)), dma((n // m, m)),
        ],
        compiler_params=pltpu.CompilerParams(
            collective_id=0, has_side_effects=True, vmem_limit_bytes=40 * 2**20),
        cost_estimate=pl.CostEstimate(
            flops=2 * n * seq_len * width * rows, bytes_accessed=60 * 2**20, transcendentals=0),
    )(g_cat, w_cat, packed)


def body(
    inputs,
    x_pre,
    bc_pre,
    dt_pre,
    gate_in,
    conv_x,
    conv_bc,
    dt_bias,
    a_log,
    d_skip,
    norm_w,
    out_grad,
    w_x,
    w_bc,
    w_dt,
):
    channels = x_pre.shape[2]
    half_width = bc_pre.shape[2]
    seq_len, model = inputs.shape[1:]
    dp_size, tensor_size = lax.axis_size("dp"), lax.axis_size("tensor")
    dp_rows = model // dp_size
    here = lax.axis_index("dp")

    def rows_of(owner):
        return lax.dynamic_slice_in_dim(inputs[0], owner * dp_rows, dp_rows, axis=1)

    rows = [rows_of(here)]
    for hop in range(1, dp_size):
        route = [(i, (i + hop) % dp_size) for i in range(dp_size)]
        rows.append(lax.ppermute(rows_of(lax.rem(here + hop, dp_size)), "dp", route))
    is_even = lax.axis_index("tensor") % 2 == 0
    bc_pre32 = bc_pre[0].astype(jnp.float32)
    own_half = state_act(bc_pre32, conv_bc).astype(jnp.bfloat16)
    far_half = swapped(own_half, "tensor", 0)
    own_float = lax.optimization_barrier(own_half).astype(jnp.float32)
    far_float = far_half.astype(jnp.float32)
    b_mat = jnp.where(is_even, own_float, far_float)[:, None, :]
    c_mat = jnp.where(is_even, far_float, own_float)[:, None, :]
    mixed_v, pullback = jax.vjp(
        state_mix,
        x_pre[0].astype(jnp.float32),
        b_mat,
        c_mat,
        dt_pre[0],
        gate_in[0].astype(jnp.float32),
        conv_x,
        dt_bias,
        a_log,
        d_skip,
    )
    upstream = out_grad[0].astype(jnp.float32)
    scaled = upstream * norm_w
    own_stats = jnp.stack([jnp.sum(mixed_v * mixed_v, axis=1), jnp.sum(scaled * mixed_v, axis=1)])
    far_stats = swapped(own_stats, "tensor", 0)
    group_stats = (own_stats + far_stats) / (2 * channels)
    inv_rms = lax.rsqrt(group_stats[0] + EPSILON)[:, None]
    grad_v = inv_rms * scaled - mixed_v * (inv_rms * inv_rms * inv_rms) * group_stats[1][:, None]
    grad_x, grad_b, grad_c, grad_dt, grad_z, grad_cx, grad_db, grad_al, grad_ds = pullback(grad_v)
    kept_grad = jnp.where(is_even, grad_b[:, 0], grad_c[:, 0])
    sent_grad = jnp.where(is_even, grad_c[:, 0], grad_b[:, 0])
    grad_own = kept_grad + swapped(sent_grad.astype(jnp.bfloat16), "tensor", 0).astype(
        sent_grad.dtype
    )
    _, pull_conv = jax.vjp(state_act, bc_pre32, conv_bc)
    grad_bcp, grad_cbc = pull_conv(grad_own)
    norm_part = jnp.sum(upstream * mixed_v * inv_rms, axis=0)
    heads = dt_pre.shape[2]
    short = jnp.pad(
        jnp.concatenate([grad_cbc.reshape(-1), grad_db, grad_al, grad_ds]),
        (0, -(4 * half_width + 3 * heads) % channels)).reshape(-1, channels)
    packed = jnp.concatenate([grad_cx, norm_part[None], short], axis=0)
    packed = jnp.pad(packed, ((0, -packed.shape[0] % 8), (0, 0)))
    width = channels + half_width + heads
    pad = -width % 128
    g_cat = jnp.concatenate(
        [grad_x.astype(jnp.bfloat16), grad_bcp.astype(jnp.bfloat16), grad_dt.astype(jnp.bfloat16),
         jnp.zeros((seq_len, pad), jnp.bfloat16)],
        axis=1,
    )
    w_cat = jnp.concatenate([w_x, w_bc, w_dt, jnp.zeros((dp_rows, pad), jnp.bfloat16)], axis=1)
    g_all, packed, moved = exchange(g_cat, w_cat, packed, dp_size, tensor_size)
    taps = grad_cx.shape[0]
    flat = packed[taps + 1 :].reshape(-1)
    cut = taps * half_width
    param_grads = (
        packed[:taps],
        flat[:cut].reshape(taps, half_width),
        flat[cut : cut + heads],
        flat[cut + heads : cut + 2 * heads],
        flat[cut + 2 * heads : cut + 3 * heads],
        packed[taps],
    )
    grad_in = moved.transpose(1, 2, 0, 3).reshape(1, seq_len, model // tensor_size)
    grad_w = lax.dot_general(
        jnp.concatenate(rows, axis=0),
        g_all.reshape(dp_size * seq_len, width + pad),
        (((0,), (0,)), ((), ())),
        preferred_element_type=jnp.float32,
    ).astype(jnp.bfloat16)[:, :width]
    return (
        grad_in,
        grad_z.astype(jnp.bfloat16)[None],
        grad_w[:, :channels],
        grad_w[:, channels : channels + half_width],
        grad_w[:, channels + half_width :],
        param_grads[0],
        param_grads[1],
        param_grads[2],
        param_grads[3],
        param_grads[4],
        param_grads[5],
    )


def solution(mesh):
    placed = (
        P("dp", None, None),
        P("dp", None, "tensor"),
        P("dp", None, "tensor"),
        P("dp", None, "tensor"),
        P("dp", None, "tensor"),
        P(None, "tensor"),
        P(None, "tensor"),
        P("tensor"),
        P("tensor"),
        P("tensor"),
        P("tensor"),
        P("dp", None, "tensor"),
        P("dp", "tensor"),
        P("dp", "tensor"),
        P("dp", "tensor"),
    )
    return jax.shard_map(
        body,
        mesh=mesh,
        in_specs=placed,
        out_specs=(
            P("dp", None, "tensor"),
            P("dp", None, "tensor"),
            P("dp", "tensor"),
            P("dp", "tensor"),
            P("dp", "tensor"),
            P(None, "tensor"),
            P(None, "tensor"),
            P("tensor"),
            P("tensor"),
            P("tensor"),
            P("tensor"),
        ),
        check_vma=False,
    )
```

```python
import jax
import jax.numpy as jnp
from jax import lax
from jax.experimental import pallas as pl
from jax.experimental.pallas import tpu as pltpu
from jax.sharding import PartitionSpec as P
import functools

EPSILON = 1e-05
PRECISE = lax.Precision.HIGHEST


def swapped(block, axis, distance):
    count = lax.axis_size(axis)
    route = []
    for low in range(count):
        high = low | 1 << distance
        if high != low and high < count:
            route += [(low, high), (high, low)]
    return lax.ppermute(block, axis, route)


def causal_conv(values, kernel):
    kernel_width = kernel.shape[0]
    seq_len = values.shape[0]
    padded = jnp.pad(values, ((kernel_width - 1, 0), (0, 0)))
    running = jnp.zeros(values.shape, jnp.float32)
    for offset in range(kernel_width):
        running = running + kernel[offset] * padded[offset : offset + seq_len]
    return running


def state_act(pre_values, kernel):
    return jax.nn.silu(causal_conv(pre_values, kernel))


def state_mix(x_pre, b_mat, c_mat, dt_pre, gate_in, conv_x, dt_bias, a_log, d_skip):
    seq_len, channels = x_pre.shape
    head_count = dt_pre.shape[1]
    groups = b_mat.shape[1]
    per_group = head_count // groups
    head_size = channels // head_count
    mixed_x = jax.nn.silu(causal_conv(x_pre, conv_x))
    step_size = jax.nn.softplus(dt_pre + dt_bias)
    decay_rate = -jnp.exp(a_log)
    log_decay = jnp.cumsum(step_size * decay_rate, axis=0).T
    scores = jnp.einsum("tgn,sgn->gts", c_mat, b_mat, precision=PRECISE)
    scores = jnp.repeat(scores, per_group, axis=0)
    causal = jnp.arange(seq_len)[:, None] >= jnp.arange(seq_len)[None, :]
    decay_mat = jnp.exp(
        jnp.where(causal[None], log_decay[:, :, None] - log_decay[:, None, :], -jnp.inf)
    )
    weights = scores * decay_mat * step_size.T[:, None, :]
    heads_x = mixed_x.reshape(seq_len, head_count, head_size)
    result = (
        jnp.einsum("hts,shp->thp", weights, heads_x, precision=PRECISE)
        + d_skip[None, :, None] * heads_x
    )
    return result.reshape(seq_len, channels) * jax.nn.silu(gate_in)


def ring_index(place, count):
    place = lax.rem(place + 2 * count, count)
    return jnp.where(place < count // 2, 2 * place, 2 * (count - 1 - place) + 1)


def exchange_kernel(
    n, m, g_ref, wx_ref, wb_ref, wd_ref, q_ref, in_ref, *rest
):
    rows_refs = rest[: n - 1]
    gwx_ref, gwb_ref, gwd_ref, sum_ref, out_ref = rest[n - 1 : n + 4]
    exchange_steps(
        n, m, g_ref, wx_ref, wb_ref, wd_ref, q_ref, in_ref, rows_refs,
        gwx_ref, gwb_ref, gwd_ref, sum_ref, out_ref, *rest[n + 4 :])


def exchange_steps(
    n, m, g_ref, wx_ref, wb_ref, wd_ref, q_ref, in_ref, rows_refs,
    gwx_ref, gwb_ref, gwd_ref, sum_ref, out_ref,
    w_ref, all_ref, rows_buf, total_buf, rows_sem, part_buf, far_buf, red_buf, q_buf,
    ring_send, ring_recv, q_send, q_recv, far_send, far_recv, red_send, red_recv,
):
    d, t = lax.axis_index("dp"), lax.axis_index("tensor")
    seq_len = g_ref.shape[0]
    part = seq_len // m
    ratio = n // m
    goal = d // ratio
    column = lax.rem(d, ratio)
    place = jnp.where(lax.rem(d, 2) == 0, d // 2, n - 1 - d // 2)
    right, left = ring_index(place + 1, n), ring_index(place - 1, n)
    right_steps = n // 2
    left_steps = n - 1 - right_steps
    depth = wx_ref.shape[0]
    cut_b = wx_ref.shape[1]
    cut_d = cut_b + wb_ref.shape[1]
    cut_end = cut_d + wd_ref.shape[1]
    loads = []
    for k in range(n):
        spot = 0
        source = in_ref.at[:, pl.ds(pl.multiple_of(d * depth, 128), depth)]
        if k:
            source = rows_refs[k - 1]
            owner = lax.rem(d - k + n, n)
            owner_place = jnp.where(lax.rem(owner, 2) == 0, owner // 2, n - 1 - owner // 2)
            apart = lax.rem(place - owner_place + n, n)
            spot = jnp.where(apart <= right_steps, 2 * apart - 1, 2 * (n - apart))
        loads.append(pltpu.make_async_copy(source, rows_buf.at[spot], rows_sem.at[k]))
        loads[-1].start()
    barrier = pltpu.get_barrier_semaphore()

    def signal(dp, tensor):
        pl.semaphore_signal(
            barrier, inc=1, device_id={"dp": dp, "tensor": tensor},
            device_id_type=pl.DeviceIdType.MESH)

    def greet_dp(k, c):
        signal(lax.rem(d + k, n), t)
        return c

    def greet_tensor(k, c):
        signal(d, lax.rem(t + k, m))
        return c

    def greet_out(s, c):
        @pl.when(jnp.logical_or(s != d, goal != t))
        def _():
            signal(s, goal)
        return c

    def greet_in(i, c):
        source, other = t * ratio + i // m, lax.rem(i, m)

        @pl.when(jnp.logical_or(source != d, other != t))
        def _():
            signal(source, other)
        return c

    lax.fori_loop(1, n, greet_dp, 0)
    lax.fori_loop(1, m, greet_tensor, 0)
    lax.fori_loop(0, n, greet_out, 0)
    lax.fori_loop(0, ratio * m, greet_in, 0)
    all_ref[0] = g_ref[...]
    q_buf[0] = q_ref[...]
    is_self = (goal == t).astype(jnp.int32)
    pl.semaphore_wait(barrier, (n - 1) + (m - 1) + n + ratio * m - 2 * is_self)

    def q_copy(k):
        return pltpu.make_async_remote_copy(
            src_ref=q_ref, dst_ref=q_buf.at[k], send_sem=q_send.at[k], recv_sem=q_recv.at[k],
            device_id={"dp": lax.rem(d + k, n)}, device_id_type=pl.DeviceIdType.MESH)

    def ring_copy(way, k):
        target = right if way == 0 else left
        held = 2 * k - 1 if way == 0 else 2 * k
        return pltpu.make_async_remote_copy(
            src_ref=all_ref.at[jnp.maximum(held, 0)],
            dst_ref=all_ref.at[held + 2],
            send_sem=ring_send.at[way, k], recv_sem=ring_recv.at[way, k],
            device_id={"dp": target}, device_id_type=pl.DeviceIdType.MESH)

    def far_copy(j, k):
        other = lax.rem(t + k, m)
        return pltpu.make_async_remote_copy(
            src_ref=part_buf.at[j, other], dst_ref=far_buf.at[j, k],
            send_sem=far_send.at[j, k], recv_sem=far_recv.at[j, k],
            device_id={"tensor": other}, device_id_type=pl.DeviceIdType.MESH)

    def out_copy(j, s):
        return pltpu.make_async_remote_copy(
            src_ref=red_buf.at[j], dst_ref=out_ref.at[column, t],
            send_sem=red_send.at[j], recv_sem=red_recv.at[column, t],
            device_id={"dp": s, "tensor": goal}, device_id_type=pl.DeviceIdType.MESH)

    def source_of(j):
        k = (j + 1) // 2
        return ring_index(jnp.where(lax.rem(j, 2) == 1, place - k, place + k), n)

    def is_remote(s):
        return jnp.logical_or(s != d, goal != t)

    ring_copy(0, 0).start()
    ring_copy(1, 0).start()

    def q_start(k, c):
        q_copy(k).start()
        return c

    lax.fori_loop(1, n, q_start, 0)
    w_ref[:, :cut_b] = wx_ref[...]
    w_ref[:, cut_b:cut_d] = wb_ref[...]
    w_ref[:, cut_d:] = jnp.zeros((depth, w_ref.shape[1] - cut_d), w_ref.dtype)
    w_ref[:, cut_d:cut_end] = wd_ref[...]
    for load in loads:
        load.wait()

    def reduce(j):
        total = part_buf[j, t].astype(jnp.float32)
        for k in range(1, m):
            far_copy(j, k).wait_recv()
            total = total + far_buf[j, k].astype(jnp.float32)
        red_buf[j] = total.astype(jnp.bfloat16)
        s = source_of(j)

        @pl.when(is_remote(s))
        def _():
            out_copy(j, s).start()

        @pl.when(jnp.logical_not(is_remote(s)))
        def _():
            out_ref[column, t] = red_buf[j]

    def step(j, c):
        k = j // 2

        @pl.when(lax.rem(j, 2) == 1)
        def _():
            ring_copy(0, k).wait_recv()

            @pl.when(k + 1 < right_steps)
            def _():
                ring_copy(0, k + 1).start()

        @pl.when(jnp.logical_and(lax.rem(j, 2) == 0, j > 0))
        def _():
            ring_copy(1, k - 1).wait_recv()

            @pl.when(k < left_steps)
            def _():
                ring_copy(1, k).start()

        product = lax.dot_general(
            all_ref[j], w_ref[...], (((1,), (1,)), ((), ())),
            preferred_element_type=jnp.float32)
        part_buf[j] = product.reshape(m, part, product.shape[1]).astype(jnp.bfloat16)
        for hop in range(1, m):
            far_copy(j, hop).start()

        @pl.when(lax.rem(j, 2) == 1)
        def _():
            grads = all_ref[pl.ds(j - 1, 2)].reshape(2 * seq_len, all_ref.shape[2])
            tile = min(256, depth)
            for low in range(0, depth, tile):
                block = rows_buf[pl.ds(j - 1, 2), :, low : low + tile]
                term = lax.dot_general(
                    block.reshape(2 * seq_len, tile), grads, (((0,), (0,)), ((), ())),
                    preferred_element_type=jnp.float32)

                @pl.when(j == 1)
                def _():
                    total_buf[low : low + tile] = term

                @pl.when(j > 1)
                def _():
                    total_buf[low : low + tile] += term

        @pl.when(j > 0)
        def _():
            reduce(j - 1)
        return c

    lax.fori_loop(0, n, step, 0)
    reduce(n - 1)

    def q_finish(k, c):
        q_copy(k).wait()
        return c

    lax.fori_loop(1, n, q_finish, 0)
    gwx_ref[...] = total_buf[:, :cut_b].astype(jnp.bfloat16)
    gwb_ref[...] = total_buf[:, cut_b:cut_d].astype(jnp.bfloat16)
    gwd_ref[...] = total_buf[:, cut_d:cut_end].astype(jnp.bfloat16)
    sum_ref[...] = jnp.sum(q_buf[...], axis=0)
    for k in range(right_steps):
        ring_copy(0, k).wait_send()
    for k in range(left_steps):
        ring_copy(1, k).wait_send()

    def drain(j, c):
        for k in range(1, m):
            far_copy(j, k).wait_send()
        s = source_of(j)

        @pl.when(is_remote(s))
        def _():
            out_copy(j, s).wait_send()
        return c

    lax.fori_loop(0, n, drain, 0)

    def arrive(i, c):
        r, other = i // m, lax.rem(i, m)

        @pl.when(jnp.logical_or(t * ratio + r != d, other != t))
        def _():
            pltpu.make_async_remote_copy(
                src_ref=red_buf.at[0], dst_ref=out_ref.at[r, other],
                send_sem=red_send.at[0], recv_sem=red_recv.at[r, other],
                device_id={"dp": t * ratio + r, "tensor": other},
                device_id_type=pl.DeviceIdType.MESH).wait_recv()
        return c

    lax.fori_loop(0, ratio * m, arrive, 0)


def exchange(g_cat, weights, packed, inputs, rows, n, m):
    seq_len, width = g_cat.shape
    depth = weights[0].shape[0]
    part = seq_len // m
    vmem = pl.BlockSpec(memory_space=pltpu.VMEM)
    dma = pltpu.SemaphoreType.DMA
    return pl.pallas_call(
        functools.partial(exchange_kernel, n, m),
        out_shape=(
            *(jax.ShapeDtypeStruct(w.shape, jnp.bfloat16) for w in weights),
            jax.ShapeDtypeStruct(packed.shape, jnp.float32),
            jax.ShapeDtypeStruct((n // m, m, part, depth), jnp.bfloat16),
        ),
        in_specs=[vmem] * 5 + [pl.BlockSpec(memory_space=pl.ANY)] * n,
        out_specs=[vmem] * 5,
        scratch_shapes=[
            pltpu.VMEM((depth, width), jnp.bfloat16),
            pltpu.VMEM((n, seq_len, width), jnp.bfloat16),
            pltpu.VMEM((n, seq_len, depth), jnp.bfloat16),
            pltpu.VMEM((depth, width), jnp.float32),
            dma((n,)),
            pltpu.VMEM((n, m, part, depth), jnp.bfloat16),
            pltpu.VMEM((n, m, part, depth), jnp.bfloat16),
            pltpu.VMEM((n, part, depth), jnp.bfloat16),
            pltpu.VMEM((n,) + packed.shape, jnp.float32),
            dma((2, n)), dma((2, n)), dma((n,)), dma((n,)),
            dma((n, m)), dma((n, m)), dma((n,)), dma((n // m, m)),
        ],
        compiler_params=pltpu.CompilerParams(
            collective_id=0, has_side_effects=True, vmem_limit_bytes=58 * 2**20),
        cost_estimate=pl.CostEstimate(
            flops=4 * n * seq_len * width * depth, bytes_accessed=60 * 2**20, transcendentals=0),
    )(g_cat, *weights, packed, inputs, *rows)


def body(
    inputs,
    x_pre,
    bc_pre,
    dt_pre,
    gate_in,
    conv_x,
    conv_bc,
    dt_bias,
    a_log,
    d_skip,
    norm_w,
    out_grad,
    w_x,
    w_bc,
    w_dt,
):
    channels = x_pre.shape[2]
    half_width = bc_pre.shape[2]
    seq_len, model = inputs.shape[1:]
    dp_size, tensor_size = lax.axis_size("dp"), lax.axis_size("tensor")
    dp_rows = model // dp_size
    here = lax.axis_index("dp")

    def rows_of(owner):
        return lax.dynamic_slice_in_dim(inputs[0], owner * dp_rows, dp_rows, axis=1)

    rows = []
    for hop in range(1, dp_size):
        route = [(i, (i + hop) % dp_size) for i in range(dp_size)]
        rows.append(lax.ppermute(rows_of(lax.rem(here + hop, dp_size)), "dp", route))
    is_even = lax.axis_index("tensor") % 2 == 0
    bc_pre32 = bc_pre[0].astype(jnp.float32)
    own_half = state_act(bc_pre32, conv_bc).astype(jnp.bfloat16)
    far_half = swapped(own_half, "tensor", 0)
    own_float = lax.optimization_barrier(own_half).astype(jnp.float32)
    far_float = far_half.astype(jnp.float32)
    b_mat = jnp.where(is_even, own_float, far_float)[:, None, :]
    c_mat = jnp.where(is_even, far_float, own_float)[:, None, :]
    mixed_v, pullback = jax.vjp(
        state_mix,
        x_pre[0].astype(jnp.float32),
        b_mat,
        c_mat,
        dt_pre[0],
        gate_in[0].astype(jnp.float32),
        conv_x,
        dt_bias,
        a_log,
        d_skip,
    )
    upstream = out_grad[0].astype(jnp.float32)
    scaled = upstream * norm_w
    own_stats = jnp.stack([jnp.sum(mixed_v * mixed_v, axis=1), jnp.sum(scaled * mixed_v, axis=1)])
    far_stats = swapped(own_stats, "tensor", 0)
    group_stats = (own_stats + far_stats) / (2 * channels)
    inv_rms = lax.rsqrt(group_stats[0] + EPSILON)[:, None]
    grad_v = inv_rms * scaled - mixed_v * (inv_rms * inv_rms * inv_rms) * group_stats[1][:, None]
    grad_x, grad_b, grad_c, grad_dt, grad_z, grad_cx, grad_db, grad_al, grad_ds = pullback(grad_v)
    kept_grad = jnp.where(is_even, grad_b[:, 0], grad_c[:, 0])
    sent_grad = jnp.where(is_even, grad_c[:, 0], grad_b[:, 0])
    grad_own = kept_grad + swapped(sent_grad.astype(jnp.bfloat16), "tensor", 0).astype(
        sent_grad.dtype
    )
    _, pull_conv = jax.vjp(state_act, bc_pre32, conv_bc)
    grad_bcp, grad_cbc = pull_conv(grad_own)
    norm_part = jnp.sum(upstream * mixed_v * inv_rms, axis=0)
    heads = dt_pre.shape[2]
    short = jnp.pad(
        jnp.concatenate([grad_cbc.reshape(-1), grad_db, grad_al, grad_ds]),
        (0, -(4 * half_width + 3 * heads) % channels)).reshape(-1, channels)
    packed = jnp.concatenate([grad_cx, norm_part[None], short], axis=0)
    packed = jnp.pad(packed, ((0, -packed.shape[0] % 8), (0, 0)))
    width = channels + half_width + heads
    pad = -width % 128
    g_cat = jnp.concatenate(
        [grad_x.astype(jnp.bfloat16), grad_bcp.astype(jnp.bfloat16), grad_dt.astype(jnp.bfloat16),
         jnp.zeros((seq_len, pad), jnp.bfloat16)],
        axis=1,
    )
    grad_wx, grad_wbc, grad_wdt, packed, moved = exchange(
        g_cat, (w_x, w_bc, w_dt), packed, inputs[0], rows, dp_size, tensor_size)
    taps = grad_cx.shape[0]
    flat = packed[taps + 1 :].reshape(-1)
    cut = taps * half_width
    param_grads = (
        packed[:taps],
        flat[:cut].reshape(taps, half_width),
        flat[cut : cut + heads],
        flat[cut + heads : cut + 2 * heads],
        flat[cut + 2 * heads : cut + 3 * heads],
        packed[taps],
    )
    grad_in = moved.transpose(1, 2, 0, 3).reshape(1, seq_len, model // tensor_size)
    return (
        grad_in,
        grad_z.astype(jnp.bfloat16)[None],
        grad_wx,
        grad_wbc,
        grad_wdt,
        param_grads[0],
        param_grads[1],
        param_grads[2],
        param_grads[3],
        param_grads[4],
        param_grads[5],
    )


def solution(mesh):
    placed = (
        P("dp", None, None),
        P("dp", None, "tensor"),
        P("dp", None, "tensor"),
        P("dp", None, "tensor"),
        P("dp", None, "tensor"),
        P(None, "tensor"),
        P(None, "tensor"),
        P("tensor"),
        P("tensor"),
        P("tensor"),
        P("tensor"),
        P("dp", None, "tensor"),
        P("dp", "tensor"),
        P("dp", "tensor"),
        P("dp", "tensor"),
    )
    return jax.shard_map(
        body,
        mesh=mesh,
        in_specs=placed,
        out_specs=(
            P("dp", None, "tensor"),
            P("dp", None, "tensor"),
            P("dp", "tensor"),
            P("dp", "tensor"),
            P("dp", "tensor"),
            P(None, "tensor"),
            P(None, "tensor"),
            P("tensor"),
            P("tensor"),
            P("tensor"),
            P("tensor"),
        ),
        check_vma=False,
    )
```

```python
import jax
import jax.numpy as jnp
from jax import lax
from jax.experimental import pallas as pl
from jax.experimental.pallas import tpu as pltpu
from jax.sharding import PartitionSpec as P
import functools

EPSILON = 1e-05
PRECISE = lax.Precision.HIGHEST


def swapped(block, axis, distance):
    count = lax.axis_size(axis)
    route = []
    for low in range(count):
        high = low | 1 << distance
        if high != low and high < count:
            route += [(low, high), (high, low)]
    return lax.ppermute(block, axis, route)


def causal_conv(values, kernel):
    kernel_width = kernel.shape[0]
    seq_len = values.shape[0]
    padded = jnp.pad(values, ((kernel_width - 1, 0), (0, 0)))
    running = jnp.zeros(values.shape, jnp.float32)
    for offset in range(kernel_width):
        running = running + kernel[offset] * padded[offset : offset + seq_len]
    return running


def state_act(pre_values, kernel):
    return jax.nn.silu(causal_conv(pre_values, kernel))


def state_mix(x_pre, b_mat, c_mat, dt_pre, gate_in, conv_x, dt_bias, a_log, d_skip):
    seq_len, channels = x_pre.shape
    head_count = dt_pre.shape[1]
    groups = b_mat.shape[1]
    per_group = head_count // groups
    head_size = channels // head_count
    mixed_x = jax.nn.silu(causal_conv(x_pre, conv_x))
    step_size = jax.nn.softplus(dt_pre + dt_bias)
    decay_rate = -jnp.exp(a_log)
    log_decay = jnp.cumsum(step_size * decay_rate, axis=0).T
    scores = jnp.einsum("tgn,sgn->gts", c_mat, b_mat, precision=PRECISE)
    scores = jnp.repeat(scores, per_group, axis=0)
    causal = jnp.arange(seq_len)[:, None] >= jnp.arange(seq_len)[None, :]
    decay_mat = jnp.exp(
        jnp.where(causal[None], log_decay[:, :, None] - log_decay[:, None, :], -jnp.inf)
    )
    weights = scores * decay_mat * step_size.T[:, None, :]
    heads_x = mixed_x.reshape(seq_len, head_count, head_size)
    result = (
        jnp.einsum("hts,shp->thp", weights, heads_x, precision=PRECISE)
        + d_skip[None, :, None] * heads_x
    )
    return result.reshape(seq_len, channels) * jax.nn.silu(gate_in)


def ring_index(place, count):
    place = lax.rem(place + 2 * count, count)
    return jnp.where(place < count // 2, 2 * place, 2 * (count - 1 - place) + 1)


def exchange_kernel(
    n, m, g_ref, wx_ref, wb_ref, wd_ref, q_ref, in_ref, *rest
):
    gwx_ref, gwb_ref, gwd_ref, sum_ref, out_ref = rest[:5]
    exchange_steps(
        n, m, g_ref, wx_ref, wb_ref, wd_ref, q_ref, in_ref,
        gwx_ref, gwb_ref, gwd_ref, sum_ref, out_ref, *rest[5:])


def exchange_steps(
    n, m, g_ref, wx_ref, wb_ref, wd_ref, q_ref, in_ref,
    gwx_ref, gwb_ref, gwd_ref, sum_ref, out_ref,
    w_ref, all_ref, rows_buf, total_buf, rows_send, rows_recv, part_buf, far_buf, red_buf, q_buf,
    ring_send, ring_recv, q_send, q_recv, far_send, far_recv, red_send, red_recv,
):
    d, t = lax.axis_index("dp"), lax.axis_index("tensor")
    seq_len = g_ref.shape[0]
    part = seq_len // m
    ratio = n // m
    goal = d // ratio
    column = lax.rem(d, ratio)
    place = jnp.where(lax.rem(d, 2) == 0, d // 2, n - 1 - d // 2)
    right, left = ring_index(place + 1, n), ring_index(place - 1, n)
    right_steps = n // 2
    left_steps = n - 1 - right_steps
    depth = wx_ref.shape[0]
    cut_b = wx_ref.shape[1]
    cut_d = cut_b + wb_ref.shape[1]
    cut_end = cut_d + wd_ref.shape[1]
    own_rows = pltpu.make_async_copy(
        in_ref.at[:, pl.ds(pl.multiple_of(d * depth, 128), depth)], rows_buf.at[0], rows_recv.at[0])
    own_rows.start()
    barrier = pltpu.get_barrier_semaphore()

    def signal(dp, tensor):
        pl.semaphore_signal(
            barrier, inc=1, device_id={"dp": dp, "tensor": tensor},
            device_id_type=pl.DeviceIdType.MESH)

    def greet_dp(k, c):
        signal(lax.rem(d + k, n), t)
        return c

    def greet_tensor(k, c):
        signal(d, lax.rem(t + k, m))
        return c

    def greet_out(s, c):
        @pl.when(jnp.logical_or(s != d, goal != t))
        def _():
            signal(s, goal)
        return c

    def greet_in(i, c):
        source, other = t * ratio + i // m, lax.rem(i, m)

        @pl.when(jnp.logical_or(source != d, other != t))
        def _():
            signal(source, other)
        return c

    lax.fori_loop(1, n, greet_dp, 0)
    lax.fori_loop(1, m, greet_tensor, 0)
    lax.fori_loop(0, n, greet_out, 0)
    lax.fori_loop(0, ratio * m, greet_in, 0)
    all_ref[0] = g_ref[...]
    q_buf[0] = q_ref[...]
    is_self = (goal == t).astype(jnp.int32)
    pl.semaphore_wait(barrier, (n - 1) + (m - 1) + n + ratio * m - 2 * is_self)

    def q_copy(k):
        return pltpu.make_async_remote_copy(
            src_ref=q_ref, dst_ref=q_buf.at[k], send_sem=q_send.at[k], recv_sem=q_recv.at[k],
            device_id={"dp": lax.rem(d + k, n)}, device_id_type=pl.DeviceIdType.MESH)

    def ring_copy(way, k):
        target = right if way == 0 else left
        held = 2 * k - 1 if way == 0 else 2 * k
        return pltpu.make_async_remote_copy(
            src_ref=all_ref.at[jnp.maximum(held, 0)],
            dst_ref=all_ref.at[held + 2],
            send_sem=ring_send.at[way, k], recv_sem=ring_recv.at[way, k],
            device_id={"dp": target}, device_id_type=pl.DeviceIdType.MESH)

    def far_copy(j, k):
        other = lax.rem(t + k, m)
        return pltpu.make_async_remote_copy(
            src_ref=part_buf.at[j, other], dst_ref=far_buf.at[j, k],
            send_sem=far_send.at[j, k], recv_sem=far_recv.at[j, k],
            device_id={"tensor": other}, device_id_type=pl.DeviceIdType.MESH)

    def out_copy(j, s):
        return pltpu.make_async_remote_copy(
            src_ref=red_buf.at[j], dst_ref=out_ref.at[column, t],
            send_sem=red_send.at[j], recv_sem=red_recv.at[column, t],
            device_id={"dp": s, "tensor": goal}, device_id_type=pl.DeviceIdType.MESH)

    def source_of(j):
        k = (j + 1) // 2
        return ring_index(jnp.where(lax.rem(j, 2) == 1, place - k, place + k), n)

    def is_remote(s):
        return jnp.logical_or(s != d, goal != t)

    ring_copy(0, 0).start()
    ring_copy(1, 0).start()

    def q_start(k, c):
        q_copy(k).start()
        return c

    lax.fori_loop(1, n, q_start, 0)
    w_ref[:, :cut_b] = wx_ref[...]
    w_ref[:, cut_b:cut_d] = wb_ref[...]
    w_ref[:, cut_d:] = jnp.zeros((depth, w_ref.shape[1] - cut_d), w_ref.dtype)
    w_ref[:, cut_d:cut_end] = wd_ref[...]
    own_rows.wait()

    def rows_copy(k):
        target = lax.rem(d + k, n)
        target_place = jnp.where(lax.rem(target, 2) == 0, target // 2, n - 1 - target // 2)
        apart = lax.rem(target_place - place + n, n)
        spot = jnp.where(apart <= right_steps, 2 * apart - 1, 2 * (n - apart))
        return pltpu.make_async_remote_copy(
            src_ref=in_ref.at[:, pl.ds(pl.multiple_of(target * depth, 128), depth)],
            dst_ref=rows_buf.at[spot], send_sem=rows_send.at[k], recv_sem=rows_recv.at[spot],
            device_id={"dp": target}, device_id_type=pl.DeviceIdType.MESH)

    def rows_wait(j):
        pltpu.make_async_remote_copy(
            src_ref=rows_buf.at[0], dst_ref=rows_buf.at[j],
            send_sem=rows_send.at[0], recv_sem=rows_recv.at[j],
            device_id={"dp": right}, device_id_type=pl.DeviceIdType.MESH).wait_recv()

    def reduce(j):
        total = part_buf[j, t].astype(jnp.float32)
        for k in range(1, m):
            far_copy(j, k).wait_recv()
            total = total + far_buf[j, k].astype(jnp.float32)
        red_buf[j] = total.astype(jnp.bfloat16)
        s = source_of(j)

        @pl.when(is_remote(s))
        def _():
            out_copy(j, s).start()

        @pl.when(jnp.logical_not(is_remote(s)))
        def _():
            out_ref[column, t] = red_buf[j]

    def step(j, c):
        k = j // 2

        @pl.when(lax.rem(j, 2) == 1)
        def _():
            ring_copy(0, k).wait_recv()

            @pl.when(k + 1 < right_steps)
            def _():
                ring_copy(0, k + 1).start()

        @pl.when(jnp.logical_and(lax.rem(j, 2) == 0, j > 0))
        def _():
            ring_copy(1, k - 1).wait_recv()

            @pl.when(k < left_steps)
            def _():
                ring_copy(1, k).start()

        product = lax.dot_general(
            all_ref[j], w_ref[...], (((1,), (1,)), ((), ())),
            preferred_element_type=jnp.float32)
        part_buf[j] = product.reshape(m, part, product.shape[1]).astype(jnp.bfloat16)
        for hop in range(1, m):
            far_copy(j, hop).start()

        @pl.when(j < n - 1)
        def _():
            rows_copy(j + 1).start()

        @pl.when(j > 0)
        def _():
            reduce(j - 1)
        return c

    lax.fori_loop(0, n, step, 0)
    reduce(n - 1)

    def weight_pair(i, c):
        j = 2 * i + 1

        @pl.when(i > 0)
        def _():
            rows_wait(j - 1)

        rows_wait(j)
        grads = all_ref[pl.ds(j - 1, 2)].reshape(2 * seq_len, all_ref.shape[2])
        tile = min(256, depth)
        for low in range(0, depth, tile):
            block = rows_buf[pl.ds(j - 1, 2), :, low : low + tile]
            term = lax.dot_general(
                block.reshape(2 * seq_len, tile), grads, (((0,), (0,)), ((), ())),
                preferred_element_type=jnp.float32)

            @pl.when(j == 1)
            def _():
                total_buf[low : low + tile] = term

            @pl.when(j > 1)
            def _():
                total_buf[low : low + tile] += term
        return c

    lax.fori_loop(0, n // 2, weight_pair, 0)

    def q_finish(k, c):
        q_copy(k).wait()
        return c

    lax.fori_loop(1, n, q_finish, 0)
    gwx_ref[...] = total_buf[:, :cut_b].astype(jnp.bfloat16)
    gwb_ref[...] = total_buf[:, cut_b:cut_d].astype(jnp.bfloat16)
    gwd_ref[...] = total_buf[:, cut_d:cut_end].astype(jnp.bfloat16)
    sum_ref[...] = jnp.sum(q_buf[...], axis=0)
    for k in range(1, n):
        rows_copy(k).wait_send()
    for k in range(right_steps):
        ring_copy(0, k).wait_send()
    for k in range(left_steps):
        ring_copy(1, k).wait_send()

    def drain(j, c):
        for k in range(1, m):
            far_copy(j, k).wait_send()
        s = source_of(j)

        @pl.when(is_remote(s))
        def _():
            out_copy(j, s).wait_send()
        return c

    lax.fori_loop(0, n, drain, 0)

    def arrive(i, c):
        r, other = i // m, lax.rem(i, m)

        @pl.when(jnp.logical_or(t * ratio + r != d, other != t))
        def _():
            pltpu.make_async_remote_copy(
                src_ref=red_buf.at[0], dst_ref=out_ref.at[r, other],
                send_sem=red_send.at[0], recv_sem=red_recv.at[r, other],
                device_id={"dp": t * ratio + r, "tensor": other},
                device_id_type=pl.DeviceIdType.MESH).wait_recv()
        return c

    lax.fori_loop(0, ratio * m, arrive, 0)


def exchange(g_cat, weights, packed, inputs, n, m):
    seq_len, width = g_cat.shape
    depth = weights[0].shape[0]
    part = seq_len // m
    vmem = pl.BlockSpec(memory_space=pltpu.VMEM)
    dma = pltpu.SemaphoreType.DMA
    return pl.pallas_call(
        functools.partial(exchange_kernel, n, m),
        out_shape=(
            *(jax.ShapeDtypeStruct(w.shape, jnp.bfloat16) for w in weights),
            jax.ShapeDtypeStruct(packed.shape, jnp.float32),
            jax.ShapeDtypeStruct((n // m, m, part, depth), jnp.bfloat16),
        ),
        in_specs=[vmem] * 5 + [pl.BlockSpec(memory_space=pl.ANY)],
        out_specs=[vmem] * 5,
        scratch_shapes=[
            pltpu.VMEM((depth, width), jnp.bfloat16),
            pltpu.VMEM((n, seq_len, width), jnp.bfloat16),
            pltpu.VMEM((n, seq_len, depth), jnp.bfloat16),
            pltpu.VMEM((depth, width), jnp.float32),
            dma((n,)),
            dma((n,)),
            pltpu.VMEM((n, m, part, depth), jnp.bfloat16),
            pltpu.VMEM((n, m, part, depth), jnp.bfloat16),
            pltpu.VMEM((n, part, depth), jnp.bfloat16),
            pltpu.VMEM((n,) + packed.shape, jnp.float32),
            dma((2, n)), dma((2, n)), dma((n,)), dma((n,)),
            dma((n, m)), dma((n, m)), dma((n,)), dma((n // m, m)),
        ],
        compiler_params=pltpu.CompilerParams(
            collective_id=0, has_side_effects=True, vmem_limit_bytes=58 * 2**20),
        cost_estimate=pl.CostEstimate(
            flops=4 * n * seq_len * width * depth, bytes_accessed=60 * 2**20, transcendentals=0),
    )(g_cat, *weights, packed, inputs)


def body(
    inputs,
    x_pre,
    bc_pre,
    dt_pre,
    gate_in,
    conv_x,
    conv_bc,
    dt_bias,
    a_log,
    d_skip,
    norm_w,
    out_grad,
    w_x,
    w_bc,
    w_dt,
):
    channels = x_pre.shape[2]
    half_width = bc_pre.shape[2]
    seq_len, model = inputs.shape[1:]
    dp_size, tensor_size = lax.axis_size("dp"), lax.axis_size("tensor")
    is_even = lax.axis_index("tensor") % 2 == 0
    bc_pre32 = bc_pre[0].astype(jnp.float32)
    own_half = state_act(bc_pre32, conv_bc).astype(jnp.bfloat16)
    far_half = swapped(own_half, "tensor", 0)
    own_float = lax.optimization_barrier(own_half).astype(jnp.float32)
    far_float = far_half.astype(jnp.float32)
    b_mat = jnp.where(is_even, own_float, far_float)[:, None, :]
    c_mat = jnp.where(is_even, far_float, own_float)[:, None, :]
    mixed_v, pullback = jax.vjp(
        state_mix,
        x_pre[0].astype(jnp.float32),
        b_mat,
        c_mat,
        dt_pre[0],
        gate_in[0].astype(jnp.float32),
        conv_x,
        dt_bias,
        a_log,
        d_skip,
    )
    upstream = out_grad[0].astype(jnp.float32)
    scaled = upstream * norm_w
    own_stats = jnp.stack([jnp.sum(mixed_v * mixed_v, axis=1), jnp.sum(scaled * mixed_v, axis=1)])
    far_stats = swapped(own_stats, "tensor", 0)
    group_stats = (own_stats + far_stats) / (2 * channels)
    inv_rms = lax.rsqrt(group_stats[0] + EPSILON)[:, None]
    grad_v = inv_rms * scaled - mixed_v * (inv_rms * inv_rms * inv_rms) * group_stats[1][:, None]
    grad_x, grad_b, grad_c, grad_dt, grad_z, grad_cx, grad_db, grad_al, grad_ds = pullback(grad_v)
    kept_grad = jnp.where(is_even, grad_b[:, 0], grad_c[:, 0])
    sent_grad = jnp.where(is_even, grad_c[:, 0], grad_b[:, 0])
    grad_own = kept_grad + swapped(sent_grad.astype(jnp.bfloat16), "tensor", 0).astype(
        sent_grad.dtype
    )
    _, pull_conv = jax.vjp(state_act, bc_pre32, conv_bc)
    grad_bcp, grad_cbc = pull_conv(grad_own)
    norm_part = jnp.sum(upstream * mixed_v * inv_rms, axis=0)
    heads = dt_pre.shape[2]
    short = jnp.pad(
        jnp.concatenate([grad_cbc.reshape(-1), grad_db, grad_al, grad_ds]),
        (0, -(4 * half_width + 3 * heads) % channels)).reshape(-1, channels)
    packed = jnp.concatenate([grad_cx, norm_part[None], short], axis=0)
    packed = jnp.pad(packed, ((0, -packed.shape[0] % 8), (0, 0)))
    width = channels + half_width + heads
    pad = -width % 128
    g_cat = jnp.concatenate(
        [grad_x.astype(jnp.bfloat16), grad_bcp.astype(jnp.bfloat16), grad_dt.astype(jnp.bfloat16),
         jnp.zeros((seq_len, pad), jnp.bfloat16)],
        axis=1,
    )
    grad_wx, grad_wbc, grad_wdt, packed, moved = exchange(
        g_cat, (w_x, w_bc, w_dt), packed, inputs[0], dp_size, tensor_size)
    taps = grad_cx.shape[0]
    flat = packed[taps + 1 :].reshape(-1)
    cut = taps * half_width
    param_grads = (
        packed[:taps],
        flat[:cut].reshape(taps, half_width),
        flat[cut : cut + heads],
        flat[cut + heads : cut + 2 * heads],
        flat[cut + 2 * heads : cut + 3 * heads],
        packed[taps],
    )
    grad_in = moved.transpose(1, 2, 0, 3).reshape(1, seq_len, model // tensor_size)
    return (
        grad_in,
        grad_z.astype(jnp.bfloat16)[None],
        grad_wx,
        grad_wbc,
        grad_wdt,
        param_grads[0],
        param_grads[1],
        param_grads[2],
        param_grads[3],
        param_grads[4],
        param_grads[5],
    )


def solution(mesh):
    placed = (
        P("dp", None, None),
        P("dp", None, "tensor"),
        P("dp", None, "tensor"),
        P("dp", None, "tensor"),
        P("dp", None, "tensor"),
        P(None, "tensor"),
        P(None, "tensor"),
        P("tensor"),
        P("tensor"),
        P("tensor"),
        P("tensor"),
        P("dp", None, "tensor"),
        P("dp", "tensor"),
        P("dp", "tensor"),
        P("dp", "tensor"),
    )
    return jax.shard_map(
        body,
        mesh=mesh,
        in_specs=placed,
        out_specs=(
            P("dp", None, "tensor"),
            P("dp", None, "tensor"),
            P("dp", "tensor"),
            P("dp", "tensor"),
            P("dp", "tensor"),
            P(None, "tensor"),
            P(None, "tensor"),
            P("tensor"),
            P("tensor"),
            P("tensor"),
            P("tensor"),
        ),
        check_vma=False,
    )
```
